256 devices in a mesh: row: 16 (over z_hi, x, core), col: 16 (over z_lo, y).
Axes of the slice: x: 4, y: 4, z: 8 (z_hi: 2, z_lo: 4; z = z_hi * 4 + z_lo), core: 2. Of those that a mesh axis runs over, the one named last changes fastest.
Arguments:
- queries: bfloat16 [131072, 768], P(('row', 'col')), may hold values from -52 to 52
- keys: bfloat16 [131072, 768], P(('row', 'col')), may hold values from -6 to 6
- values: bfloat16 [131072, 768], P(('row', 'col')), may hold values from -6 to 6
- out_weight: bfloat16 [768, 768], replicated, may hold values from -0.21875 to 0.21875
Outputs:
- layer_out: bfloat16 [131072, 768], P(('row', 'col'))
The draws below stay inside these ranges and needn't reach their ends.
All inputs are finite; a program needn't handle non-finite values.
Results may differ from the reference program's by a relative error of at most 0.0015.
The reference program's roundings to bfloat16 on the way count: a program that leaves them out, or rounds other values in their place, can miss the bound.
Values may be sent and summed in bfloat16 or wider, within the bound.
No kernel may reach another device: no remote copies, remote signals or barrier semaphores. Data moves between devices by JAX's collectives and lax.ppermute only.
A program may use at most 64 MiB of HBM per device.

```python
import jax
import jax.numpy as jnp
from jax import lax

D = 768
HEADS = 12
TOK_DEV = 512
TOKENS = 131072
N_ROW = 16
N_COL = 16


def draw_keys(key, part):
    key = jax.random.fold_in(key, 3)
    return jnp.clip(jax.random.normal(key, (TOKENS, D), jnp.float32), -6.0, 6.0).astype(jnp.bfloat16)


def draw_queries(key, part):
    key = jax.random.fold_in(key, 7)
    return jnp.clip(jax.random.normal(key, (TOKENS, D), jnp.float32), -6.0, 6.0).astype(jnp.bfloat16)


def level_of(own_key, dims, cuts, smallest, high):
    def one(position, shards_of):
        steps = jax.random.uniform(jax.random.fold_in(jax.random.fold_in(own_key, 6), position), (shards_of,), jnp.float32, smallest / len(cuts), high / len(cuts))
        return jnp.repeat(jnp.exp(steps), dims[position] // shards_of).reshape((-1,) + (1,) * (len(dims) - position - 1))

    loudness = one(*cuts[0])
    for cut in cuts[1:]:
        loudness = loudness * one(*cut)
    return loudness


def centred(rng, extent, scale, reach, shards=(), dtype=jnp.bfloat16):
    drawn = scale * jax.random.normal(rng, extent, jnp.float32)
    if shards:
        drawn = drawn * level_of(rng, extent, shards, -0.22, 0.18)
    return jnp.clip(drawn, -reach, reach).astype(dtype)


def setup_inputs(seed: int = 0) -> dict:
    streams_of = jax.random.split(jax.random.key(seed), 5)
    return {
        "queries": draw_queries(jax.random.fold_in(streams_of[4], 71), 0),
        "keys": draw_keys(jax.random.fold_in(streams_of[4], 71), 0),
        "values": centred(streams_of[2], (TOKENS, D), 1.0, 6.0, ((0, 256),)),
        "out_weight": centred(streams_of[3], (D, D), D ** -0.5, 0.21875),
    }


def attend(query_rows, key_rows, value_rows):
    score_scale = query_rows.shape[-1] ** -0.5
    scores = jnp.einsum("qhd,khd->hqk", query_rows.astype(jnp.float32), key_rows.astype(jnp.float32), precision=lax.Precision.HIGHEST) * score_scale
    row_max = jnp.max(scores, axis=-1, keepdims=True)
    exponent = jnp.exp(scores - row_max)
    totals = jnp.sum(exponent, axis=-1)
    weights = lax.optimization_barrier(exponent.astype(jnp.bfloat16)).astype(jnp.float32)
    summed = jnp.einsum("hqk,khd->qhd", weights, value_rows.astype(jnp.float32), precision=lax.Precision.HIGHEST)
    outputs = summed / jnp.transpose(totals)[:, :, None]
    return outputs, jnp.transpose(row_max[..., 0] + jnp.log(totals))


def spread(compact, period, offsets, filler):
    chosen = jnp.arange(period)[:, None] == offsets[None, :]
    if compact.ndim == 3:
        chosen = chosen[None, :, :, None]
    else:
        chosen = chosen[None, :, :]
    placed = jnp.where(chosen, compact[:, None], filler)
    return placed.reshape((-1,) + compact.shape[1:])


def combine(pieces):
    row_max = pieces[0][1]
    for piece in pieces[1:]:
        row_max = jnp.maximum(row_max, piece[1])
    numer = jnp.zeros_like(pieces[0][0])
    denom = jnp.zeros_like(row_max)
    for piece in pieces:
        factor = jnp.exp(piece[1] - row_max)
        numer = numer + factor[:, :, None] * piece[0]
        denom = denom + factor
    return numer / denom[:, :, None]


def reference(queries, keys, values, out_weight):
    head_dim = D // HEADS
    top_period = N_ROW * N_COL
    head_ids = jnp.arange(HEADS)
    first_offsets = head_ids % N_COL
    second_offsets = head_ids % top_period

    def local_view(source):
        return source.reshape(TOKENS // TOK_DEV, TOK_DEV, HEADS, head_dim)

    def attend_tuple(triple):
        return attend(triple[0], triple[1], triple[2])

    out_zero, lse_zero = lax.map(attend_tuple, (local_view(queries), local_view(keys), local_view(values)))

    def select_segment(source):
        return source.reshape(N_ROW, TOK_DEV, N_COL, HEADS, head_dim)[:, :, first_offsets, head_ids]

    out_one, lse_one = lax.map(attend_tuple, (select_segment(queries), select_segment(keys), select_segment(values)))

    def select_sequence(source):
        return source.reshape(TOKENS // top_period, top_period, HEADS, head_dim)[:, second_offsets, head_ids]

    out_two, lse_two = attend(select_sequence(queries), select_sequence(keys), select_sequence(values))
    seg_len = TOK_DEV * N_COL

    def per_block(items):
        block_zero, block_lse_zero, block_one, block_lse_one, block_two, block_lse_two = items
        first_full = spread(block_one, N_COL, first_offsets, 0.0)
        first_lse = spread(block_lse_one, N_COL, first_offsets, -jnp.inf)
        second_full = spread(block_two, top_period, second_offsets, 0.0)
        second_lse = spread(block_lse_two, top_period, second_offsets, -jnp.inf)
        mixed = combine([(block_zero, block_lse_zero), (first_full, first_lse), (second_full, second_lse)])
        mixed = mixed.astype(jnp.bfloat16).reshape(seg_len, D)
        return jnp.dot(mixed, out_weight, preferred_element_type=jnp.float32).astype(jnp.bfloat16)

    result = lax.map(per_block, (
        out_zero.reshape(N_ROW, seg_len, HEADS, head_dim),
        lse_zero.reshape(N_ROW, seg_len, HEADS),
        out_one,
        lse_one,
        out_two.reshape(N_ROW, TOK_DEV // N_ROW, HEADS, head_dim),
        lse_two.reshape(N_ROW, TOK_DEV // N_ROW, HEADS),
    ))
    return result.reshape(TOKENS, D)
```

```python
import jax
import jax.numpy as jnp
from jax import lax
from jax.experimental import pallas as pl
from jax.experimental.pallas import tpu as pltpu
from jax.sharding import PartitionSpec as P

HEADS = 12
F32 = jnp.float32
BF16 = jnp.bfloat16
NT = (((1,), (1,)), ((), ()))


def lane_is_low(shape):
    return lax.broadcasted_iota(jnp.int32, shape, len(shape) - 1) < 64


def swap(block):
    return pltpu.roll(block, 64, block.ndim - 1)


def chosen_lanes(period, width):
    offset = lax.broadcasted_iota(jnp.int32, (period, width), 0)
    head = lax.broadcasted_iota(jnp.int32, (period, width), 1) // 64
    return offset == head


def pack_kernel(period, q_ref, k_ref, v_ref, x_ref):
    rows, width = q_ref.shape
    groups = rows // period
    keep = chosen_lanes(period, width).astype(BF16)
    member = (
        lax.broadcasted_iota(jnp.int32, (groups, rows), 1) // period
        == lax.broadcasted_iota(jnp.int32, (groups, rows), 0)
    ).astype(BF16)

    def pick(ref):
        kept = ref[...].reshape(groups, period, width) * keep[None]
        return jnp.dot(member, kept.reshape(rows, width), preferred_element_type=F32)

    q, k, v = pick(q_ref), pick(k_ref), pick(v_ref)
    low = lane_is_low((groups, 128))
    low_half = lane_is_low((groups // 2, 128))
    for pair in range(HEADS // 2):
        lanes = slice(pair * 128, pair * 128 + 128)
        qb, kb, vb = q[:, lanes], k[:, lanes], v[:, lanes]
        top, bottom = vb[: groups // 2], vb[groups // 2 :]
        x_ref[2 * pair, :groups] = jnp.where(low, qb, swap(kb)).astype(BF16)
        x_ref[2 * pair, groups:] = jnp.where(low_half, top, swap(bottom)).astype(BF16)
        x_ref[2 * pair + 1, :groups] = jnp.where(low, swap(qb), kb).astype(BF16)
        x_ref[2 * pair + 1, groups:] = jnp.where(low_half, swap(top), bottom).astype(BF16)
    for rest in range(HEADS, x_ref.shape[0]):
        x_ref[rest] = jnp.zeros(x_ref.shape[1:], BF16)


def middle_kernel(y_ref, z_ref):
    y = y_ref[...].astype(F32)
    first, second, val = y[:, 0, :], y[:, 16, :], y[:, 32, :]
    low = lane_is_low(first.shape)
    top = jnp.where(low, swap(first), swap(val)).astype(BF16)
    bottom = jnp.where(low, swap(second), val).astype(BF16)
    both = jnp.concatenate([top, bottom], axis=0)
    for i in range(z_ref.shape[0]):
        z_ref[i] = both


def soft(scores):
    top = jnp.max(scores, axis=-1, keepdims=True)
    weights = jnp.exp((scores - top) * 0.125)
    total = jnp.sum(weights, axis=-1, keepdims=True)
    return weights.astype(BF16), total, top * 0.125 + jnp.log(total)


def merge(out_a, lse_a, out_b, lse_b):
    top = jnp.maximum(lse_a, lse_b)
    wa, wb = jnp.exp(lse_a - top), jnp.exp(lse_b - top)
    total = wa + wb
    return (wa * out_a + wb * out_b) / total, top + jnp.log(total)


def shared_kernel(y_ref, z_ref, ret_ref):
    n, _, _ = y_ref.shape
    qk = y_ref[:, :32, :].reshape(n * 32, 128).astype(F32)
    low = lane_is_low(qk.shape)
    query = jnp.where(low, qk, 0.0).astype(BF16)
    key = swap(qk).astype(BF16)
    val = y_ref[:, 32:, :].astype(F32).reshape(n * 16, 128)
    other = swap(val).reshape(n, 16, 128)
    val = jnp.concatenate([val.reshape(n, 16, 128), other], axis=1).reshape(n * 32, 128).astype(BF16)
    scores = lax.dot_general(query, key, NT, preferred_element_type=F32)
    probs, total, lse = soft(scores)
    out = jnp.dot(probs, val, preferred_element_type=F32) / total
    ret_ref[...] = jnp.where(low, out, lse).reshape(n, 32, 128)

    y = y_ref[...].astype(F32)
    q2 = jnp.concatenate([y[:, 0, :], y[:, 16, :]], axis=0)
    low2 = lane_is_low(q2.shape)
    q2 = jnp.where(low2, q2, 0.0).astype(BF16)
    kv = z_ref[...].reshape(-1, 128)
    scores2 = lax.dot_general(q2, kv, NT, preferred_element_type=F32)
    probs2, total2, lse2 = soft(scores2)
    out2 = swap(jnp.dot(probs2, kv, preferred_element_type=F32) / total2)
    for i in range(2):
        old = ret_ref[:, 16 * i, :]
        part = slice(n * i, n * i + n)
        lse_old = swap(old)
        mixed, lse_new = merge(old, lse_old, out2[part], lse2[part])
        lown = lane_is_low(old.shape)
        ret_ref[:, 16 * i, :] = jnp.where(lown, mixed, swap(lse_new))


def local_kernel(q_ref, k_ref, v_ref, o_ref, s_ref, out_scr, lse_scr):
    pair = pl.program_id(0)
    q, k, v = q_ref[...], k_ref[...], v_ref[...]
    low = lane_is_low(q.shape)
    outs, lses = [], []
    for half in range(2):
        query = jnp.where(low == (half == 0), q, jnp.zeros_like(q))
        scores = lax.dot_general(query, k, NT, preferred_element_type=F32)
        probs, total, lse = soft(scores)
        outs.append(jnp.dot(probs, v, preferred_element_type=F32) / total)
        lses.append(lse)
    out = jnp.where(low, outs[0], outs[1])
    o_ref[...] = out.astype(BF16)
    out_scr[...] = out
    lse_scr[...] = jnp.where(low, lses[0], lses[1])
    for half in range(2):
        rows = pl.ds(2 * pair + half, s_ref.shape[1], stride=16)
        o, l = out_scr[rows, :], lse_scr[rows, :]
        lowr = lane_is_low(o.shape)
        if half == 0:
            s_ref[half] = jnp.where(lowr, o, swap(l))
        else:
            s_ref[half] = jnp.where(lowr, swap(o), l)


def finish_kernel(period, o_ref, s_ref, r_ref, w_ref, out_ref):
    rows, width = o_ref.shape
    groups = rows // period
    low = lane_is_low((groups, 128))
    blocks = []
    for pair in range(HEADS // 2):
        halves = []
        for half in range(2):
            a, b = s_ref[2 * pair + half], r_ref[2 * pair + half]
            halves.append(merge(a, swap(a), b, swap(b))[0])
        blocks.append(jnp.where(low, halves[0], swap(halves[1])).astype(BF16))
    merged = jnp.concatenate(blocks, axis=1)
    member = (
        lax.broadcasted_iota(jnp.int32, (rows, groups), 0) // period
        == lax.broadcasted_iota(jnp.int32, (rows, groups), 1)
    ).astype(BF16)
    spread = jnp.dot(member, merged, preferred_element_type=F32).reshape(groups, period, width)
    keep = chosen_lanes(period, width)[None]
    local = o_ref[...].astype(F32).reshape(groups, period, width)
    mixed = jnp.where(keep, spread, local).reshape(rows, width).astype(BF16)
    out_ref[...] = jnp.dot(mixed, w_ref[...], preferred_element_type=F32).astype(BF16)


def shards(queries, keys, values, out_weight):
    n_row, n_col = lax.axis_size("row"), lax.axis_size("col")
    rows, width = queries.shape
    groups = rows // n_col
    params = pltpu.CompilerParams(vmem_limit_bytes=48 * 1024 * 1024)

    def call(kernel, out, **kw):
        return pl.pallas_call(kernel, out_shape=out, compiler_params=params, **kw)

    shape = jax.ShapeDtypeStruct
    packed = call(
        lambda *refs: pack_kernel(n_col, *refs), shape((n_col, groups * 3 // 2, 128), BF16)
    )(queries, keys, values)
    mine = lax.all_to_all(packed, "col", 0, 0)
    top_own = call(middle_kernel, shape((n_row, 2 * n_col, 128), BF16))(mine)
    top_all = lax.all_to_all(top_own, "row", 0, 0)
    block = pl.BlockSpec((rows, 128), lambda i: (0, i))
    local, picked = call(
        local_kernel,
        (shape((rows, width), BF16), shape((HEADS, groups, 128), F32)),
        grid=(HEADS // 2,),
        in_specs=[block] * 3,
        out_specs=(block, pl.BlockSpec((2, groups, 128), lambda i: (i, 0, 0))),
        scratch_shapes=[pltpu.VMEM((rows, 128), F32)] * 2,
    )(queries, keys, values)
    ret = call(shared_kernel, shape((n_col, groups, 128), F32))(mine, top_all)
    back = lax.all_to_all(ret, "col", 0, 0)
    return call(
        lambda *refs: finish_kernel(n_col, *refs), shape((rows, width), BF16)
    )(local, picked, back, out_weight)


def solution(mesh):
    placed = (P(("row", "col"), None), P(("row", "col"), None), P(("row", "col"), None), P())
    return jax.shard_map(
        shards, mesh=mesh, in_specs=placed, out_specs=P(("row", "col"), None), check_vma=False
    )
```

```python
import jax
import jax.numpy as jnp
from jax import lax
from jax.experimental import pallas as pl
from jax.experimental.pallas import tpu as pltpu
from jax.sharding import PartitionSpec as P

HEADS = 12
F32 = jnp.float32
BF16 = jnp.bfloat16
NT = (((1,), (1,)), ((), ()))


def lane_is_low(shape):
    return lax.broadcasted_iota(jnp.int32, shape, len(shape) - 1) < 64


def swap(block):
    return pltpu.roll(block, 64, block.ndim - 1)


def chosen_lanes(period, width):
    offset = lax.broadcasted_iota(jnp.int32, (period, width), 0)
    head = lax.broadcasted_iota(jnp.int32, (period, width), 1) // 64
    return offset == head


def slot_of(head, n_row, n_col):
    moved = lax.div(lax.axis_index("row"), n_row // 2) * (n_col // 2)
    return lax.rem(head + moved, n_col)


def pack_kernel(period, n_row, q_hbm, k_hbm, v_hbm, x_ref, buf, sem):
    rows, width = q_hbm.shape
    copies = [
        pltpu.make_async_copy(hbm, buf.at[i], sem.at[i])
        for i, hbm in enumerate((q_hbm, k_hbm, v_hbm))
    ]
    for copy in copies:
        copy.start()
    groups = rows // period
    keep = chosen_lanes(period, width).astype(BF16)
    member = (
        lax.broadcasted_iota(jnp.int32, (groups, rows), 1) // period
        == lax.broadcasted_iota(jnp.int32, (groups, rows), 0)
    ).astype(BF16)

    def pick(i):
        copies[i].wait()
        kept = buf[i].reshape(groups, period, width) * keep[None]
        return jnp.dot(member, kept.reshape(rows, width), preferred_element_type=F32)

    q, k, v = pick(0), pick(1), pick(2)
    low = lane_is_low((groups, 128))
    low_half = lane_is_low((groups // 2, 128))
    for pair in range(HEADS // 2):
        lanes = slice(pair * 128, pair * 128 + 128)
        qb, kb, vb = q[:, lanes], k[:, lanes], v[:, lanes]
        top, bottom = vb[: groups // 2], vb[groups // 2 :]
        even, odd = slot_of(2 * pair, n_row, period), slot_of(2 * pair + 1, n_row, period)
        x_ref[even, :groups] = jnp.where(low, qb, swap(kb)).astype(BF16)
        x_ref[even, groups:] = jnp.where(low_half, top, swap(bottom)).astype(BF16)
        x_ref[odd, :groups] = jnp.where(low, swap(qb), kb).astype(BF16)
        x_ref[odd, groups:] = jnp.where(low_half, swap(top), bottom).astype(BF16)
    for rest in range(HEADS, x_ref.shape[0]):
        x_ref[slot_of(rest, n_row, period)] = jnp.zeros(x_ref.shape[1:], BF16)


def middle_kernel(y_ref, z_ref):
    y = y_ref[...].astype(F32)
    first, second, val = y[:, 0, :], y[:, 16, :], y[:, 32, :]
    low = lane_is_low(first.shape)
    top = jnp.where(low, swap(first), swap(val)).astype(BF16)
    bottom = jnp.where(low, swap(second), val).astype(BF16)
    both = jnp.concatenate([top, bottom], axis=0)
    for i in range(z_ref.shape[0]):
        z_ref[i] = both


def soft(scores):
    top = jnp.max(scores, axis=-1, keepdims=True)
    weights = jnp.exp((scores - top) * 0.125)
    total = jnp.sum(weights, axis=-1, keepdims=True)
    return weights.astype(BF16), total, top * 0.125 + jnp.log(total)


def merge(out_a, lse_a, out_b, lse_b):
    top = jnp.maximum(lse_a, lse_b)
    wa, wb = jnp.exp(lse_a - top), jnp.exp(lse_b - top)
    total = wa + wb
    return (wa * out_a + wb * out_b) / total, top + jnp.log(total)


def segment_kernel(y_ref, out_ref):
    n, _, _ = y_ref.shape
    qk = y_ref[:, :32, :].reshape(n * 32, 128).astype(F32)
    low = lane_is_low(qk.shape)
    query = jnp.where(low, qk, 0.0).astype(BF16)
    key = swap(qk).astype(BF16)
    val = y_ref[:, 32:, :].astype(F32).reshape(n * 16, 128)
    other = swap(val).reshape(n, 16, 128)
    val = jnp.concatenate([val.reshape(n, 16, 128), other], axis=1).reshape(n * 32, 128).astype(BF16)
    scores = lax.dot_general(query, key, NT, preferred_element_type=F32)
    probs, total, lse = soft(scores)
    out = jnp.dot(probs, val, preferred_element_type=F32) / total
    out_ref[...] = jnp.where(low, out, lse).reshape(n, 32, 128)


def sequence_kernel(y_ref, z_ref, o_ref, ret_ref):
    n = y_ref.shape[0]
    q2 = jnp.concatenate([y_ref[:, 16 * i : 16 * i + 16, :].astype(F32)[:, 0, :] for i in range(2)], axis=0)
    q2 = jnp.where(lane_is_low(q2.shape), q2, 0.0).astype(BF16)
    kv = z_ref[...].reshape(-1, 128)
    scores = lax.dot_general(q2, kv, NT, preferred_element_type=F32)
    probs, total, lse = soft(scores)
    out = swap(jnp.dot(probs, kv, preferred_element_type=F32) / total)
    row = lax.broadcasted_iota(jnp.int32, (n, 16, 128), 1)
    halves = []
    for i in range(2):
        old = o_ref[:, 16 * i : 16 * i + 16, :]
        first = old[:, 0, :]
        part = slice(n * i, n * i + n)
        mixed, lse_new = merge(first, swap(first), out[part], lse[part])
        first = jnp.where(lane_is_low(first.shape), mixed, swap(lse_new))
        halves.append(jnp.where(row == 0, first[:, None, :], old))
    low, high = halves
    ret_ref[:, :16, :] = jnp.where(lane_is_low(low.shape), low, swap(high))
    quarter = lax.broadcasted_iota(jnp.int32, (n, 8, 128), 2) // 32
    ret_ref[:, 16:, :] = jnp.where(
        quarter < 2,
        jnp.where(quarter == 0, low[:, :8, 64:65], low[:, 8:, 64:65]),
        jnp.where(quarter == 2, high[:, :8, 64:65], high[:, 8:, 64:65]),
    )


def split(x):
    def leading(y):
        scaled = y * 65537.0
        return scaled - (scaled - y)

    high = leading(x)
    rest = x - high
    mid = leading(rest)
    return high, mid, rest - mid


def local_kernel(start, q_hbm, k_hbm, v_hbm, *rest):
    o_ref, buf, sem, out_scr, lse_scr = rest[-5:]
    step, steps = pl.program_id(0), pl.num_programs(0)
    rows = q_hbm.shape[0]
    groups = rows // 16

    def copies(pair):
        lanes, slot = pl.ds(pl.multiple_of((start + pair) * 128, 128), 128), lax.rem(pair, 2)
        return [
            pltpu.make_async_copy(hbm.at[:, lanes], buf.at[slot, i], sem.at[slot, i])
            for i, hbm in enumerate((q_hbm, k_hbm, v_hbm))
        ]

    @pl.when(step == 0)
    def _():
        for copy in copies(step):
            copy.start()

    @pl.when(step + 1 < steps)
    def _():
        for copy in copies(step + 1):
            copy.start()

    for copy in copies(step):
        copy.wait()
    slot = lax.rem(step, 2)
    q, k, v = buf[slot, 0], buf[slot, 1], buf[slot, 2]
    low = lane_is_low(q.shape)
    outs, lses = [], []
    for half in range(2):
        query = jnp.where(low == (half == 0), q, jnp.zeros_like(q))
        scores = lax.dot_general(query, k, NT, preferred_element_type=F32)
        probs, total, lse = soft(scores)
        outs.append(jnp.dot(probs, v, preferred_element_type=F32) / total)
        lses.append(lse)
    out = jnp.where(low, outs[0], outs[1])
    out_scr[...] = out
    lse_scr[...] = jnp.where(low, lses[0], lses[1])
    o_ref[:rows, :] = out.astype(BF16)
    lowr = lane_is_low((groups, 128))
    even = pl.ds(2 * (start + step), groups, stride=16)
    odd = pl.ds(2 * (start + step) + 1, groups, stride=16)
    at = rows
    for scr in (out_scr, lse_scr):
        for piece in split(jnp.where(lowr, scr[even, :], scr[odd, :])):
            o_ref[at : at + groups, :] = piece.astype(BF16)
            at += groups


def finish_kernel(period, n_row, local, r_ref, w_ref, out_hbm, buf, out_sem):
    rows, width = out_hbm.shape
    groups = rows // period
    n = r_ref.shape[0]
    low = lane_is_low((groups, 128))
    remote = []
    for pair in range(HEADS // 2):
        back = [r_ref[slot_of(2 * pair + half, n_row, n)] for half in range(2)]
        outs = [b[: groups // 2] for b in back]
        lses = [b[groups // 2 :] for b in back]
        lse = [
            jnp.concatenate([b[:, 32 * i : 32 * i + 1] for i in range(4)], axis=0) for b in lses
        ]
        low_half = lane_is_low(outs[0].shape)
        out_b = jnp.concatenate(
            [jnp.where(low_half, outs[0], swap(outs[1])), jnp.where(low_half, swap(outs[0]), outs[1])], axis=0
        )
        remote.append((out_b, jnp.where(low, lse[0], lse[1])))
    blocks = []
    for pair in range(HEADS // 2):
        lanes = slice(pair * 128, pair * 128 + 128)
        pieces = [
            local[rows + i * groups : rows + (i + 1) * groups, lanes].astype(F32) for i in range(6)
        ]
        out_a, lse_a = (pieces[i] + pieces[i + 1] + pieces[i + 2] for i in (0, 3))
        blocks.append(merge(out_a, lse_a, *remote[pair])[0])
    merged = jnp.concatenate(blocks, axis=1)
    keep = chosen_lanes(period, width)[None]
    own = local[:rows, :].astype(F32).reshape(groups, period, width)
    mixed = jnp.where(keep, merged[:, None, :], own).reshape(rows, width).astype(BF16)
    chunks = buf.shape[0]
    wide = width // chunks
    copies = []
    for c in range(chunks):
        part = pl.ds(c * wide, wide)
        buf[c] = jnp.dot(mixed, w_ref[:, part], preferred_element_type=F32).astype(BF16)
        copy = pltpu.make_async_copy(buf.at[c], out_hbm.at[:, part], out_sem.at[c])
        copy.start()
        copies.append(copy)
    for copy in copies:
        copy.wait()


def shards(queries, keys, values, out_weight):
    n_row, n_col = lax.axis_size("row"), lax.axis_size("col")
    rows, width = queries.shape
    groups = rows // n_col
    shape = jax.ShapeDtypeStruct

    def call(kernel, out, mib=16, **kw):
        params = pltpu.CompilerParams(vmem_limit_bytes=mib * 1024 * 1024)
        return pl.pallas_call(kernel, out_shape=out, compiler_params=params, **kw)

    anywhere = pl.BlockSpec(memory_space=pl.ANY)
    distant = pl.BlockSpec(memory_space=pltpu.HBM)
    whole = pl.BlockSpec(memory_space=pltpu.VMEM)
    packed = call(
        lambda *refs: pack_kernel(n_col, n_row, *refs),
        shape((n_col, groups * 3 // 2, 128), BF16),
        mib=56,
        in_specs=[distant] * 3,
        scratch_shapes=[pltpu.VMEM((3, rows, width), BF16), pltpu.SemaphoreType.DMA((3,))],
    )(queries, keys, values)
    def local(start, count, inputs, aliases):
        pairs = rows * rows * 2 * count
        return call(
            lambda *refs: local_kernel(start, *refs),
            shape((rows + 6 * groups, width), BF16),
            mib=54,
            grid=(count,),
            in_specs=[distant] * 3 + [anywhere] * (len(inputs) - 3),
            out_specs=pl.BlockSpec((rows + 6 * groups, 128), lambda i: (0, start + i)),
            scratch_shapes=[
                pltpu.VMEM((2, 3, rows, 128), BF16),
                pltpu.SemaphoreType.DMA((2, 3)),
                pltpu.VMEM((rows, 128), F32),
                pltpu.VMEM((rows, 128), F32),
            ],
            input_output_aliases=aliases,
            cost_estimate=pl.CostEstimate(
                flops=pairs * 1024, bytes_accessed=count * rows * 128 * 10, transcendentals=pairs
            ),
        )(*inputs)

    inputs = (queries, keys, values)
    packed, *inputs = lax.optimization_barrier((packed, *inputs))
    mine = lax.all_to_all(packed, "col", 0, 0)
    early = HEADS // 4
    first = local(0, early, inputs, {})
    mine, first = lax.optimization_barrier((mine, first))
    top_own = call(middle_kernel, shape((n_row, 2 * n_col, 128), BF16))(mine)
    top_own, mine, first, *inputs = lax.optimization_barrier((top_own, mine, first, *inputs))
    owners = [
        [r * n_col + (c + 2 * r // n_row * (n_col // 2)) % n_col for r in range(n_row)]
        for c in range(n_col)
    ]
    top_all = lax.all_to_all(top_own, ("row", "col"), 0, 0, axis_index_groups=owners)
    second = local(early, HEADS // 2 - early, (*inputs, first), {3: 0})
    mine, second = lax.optimization_barrier((mine, second))
    segment = call(segment_kernel, shape((n_col, groups, 128), F32))(mine)
    top_all, segment = lax.optimization_barrier((top_all, segment))
    ret = call(
        sequence_kernel,
        shape((n_col, groups * 3 // 4, 128), F32),
        cost_estimate=pl.CostEstimate(flops=10**10, bytes_accessed=10**6, transcendentals=0),
    )(mine, top_all, segment)
    back = lax.all_to_all(ret, "col", 0, 0)
    return call(
        lambda *refs: finish_kernel(n_col, n_row, *refs),
        shape((rows, width), BF16),
        in_specs=[whole] * 3,
        out_specs=anywhere,
        scratch_shapes=[pltpu.VMEM((3, rows, width // 3), BF16), pltpu.SemaphoreType.DMA((3,))],
    )(second, back, out_weight)


def solution(mesh):
    placed = (P(("row", "col"), None), P(("row", "col"), None), P(("row", "col"), None), P())
    return jax.shard_map(
        shards, mesh=mesh, in_specs=placed, out_specs=P(("row", "col"), None), check_vma=False
    )
```

```python
import jax
import jax.numpy as jnp
from jax import lax
from jax.experimental import pallas as pl
from jax.experimental.pallas import tpu as pltpu
from jax.sharding import PartitionSpec as P

HEADS = 12
LOG2E = 1.4426950408889634
LSE_LANE = 125
F32 = jnp.float32
BF16 = jnp.bfloat16
NT = (((1,), (1,)), ((), ()))


def lane_is_low(shape):
    return lax.broadcasted_iota(jnp.int32, shape, len(shape) - 1) < 64


def swap(block):
    return pltpu.roll(block, 64, block.ndim - 1)


def chosen_lanes(period, width):
    offset = lax.broadcasted_iota(jnp.int32, (period, width), 0)
    head = lax.broadcasted_iota(jnp.int32, (period, width), 1) // 64
    return offset == head


def slot_of(head, n_row, n_col):
    side = int(n_col**0.5)
    upper = lax.div(lax.axis_index("row"), n_row // 2)
    z = head // side
    return (z + upper * (side - 1 - 2 * z)) * side + head % side


def pack_kernel(period, n_row, q_hbm, k_hbm, v_hbm, x_ref, buf, sem):
    rows, width = q_hbm.shape
    copies = [
        pltpu.make_async_copy(hbm, buf.at[i], sem.at[i])
        for i, hbm in enumerate((q_hbm, k_hbm, v_hbm))
    ]
    for copy in copies:
        copy.start()
    groups = rows // period
    keep = chosen_lanes(period, width).astype(BF16)
    member = (
        lax.broadcasted_iota(jnp.int32, (groups, rows), 1) // period
        == lax.broadcasted_iota(jnp.int32, (groups, rows), 0)
    ).astype(BF16)

    def pick(i):
        copies[i].wait()
        kept = buf[i].reshape(groups, period, width) * keep[None]
        return jnp.dot(member, kept.reshape(rows, width), preferred_element_type=F32)

    q, k = pick(0), pick(1)
    low = lane_is_low((groups, 128))
    low_half = lane_is_low((groups // 2, 128))
    pairs = [
        (slice(i * 128, i * 128 + 128), slot_of(2 * i, n_row, period), slot_of(2 * i + 1, n_row, period))
        for i in range(HEADS // 2)
    ]
    for lanes, even, odd in pairs:
        qb, kb = q[:, lanes], k[:, lanes]
        x_ref[even, :groups] = jnp.where(low, qb, swap(kb)).astype(BF16)
        x_ref[odd, :groups] = jnp.where(low, swap(qb), kb).astype(BF16)
    v = pick(2)
    for lanes, even, odd in pairs:
        top, bottom = v[: groups // 2, lanes], v[groups // 2 :, lanes]
        x_ref[even, groups:] = jnp.where(low_half, top, swap(bottom)).astype(BF16)
        x_ref[odd, groups:] = jnp.where(low_half, swap(top), bottom).astype(BF16)
    for rest in range(HEADS, x_ref.shape[0]):
        x_ref[slot_of(rest, n_row, period)] = jnp.zeros(x_ref.shape[1:], BF16)


def middle_kernel(y_ref, z_ref):
    y = y_ref[...].astype(F32)
    first, second, val = y[:, 0, :], y[:, 16, :], y[:, 32, :]
    low = lane_is_low(first.shape)
    top = jnp.where(low, swap(first), swap(val)).astype(BF16)
    bottom = jnp.where(low, swap(second), val).astype(BF16)
    both = jnp.concatenate([top, bottom], axis=0)
    for i in range(z_ref.shape[0]):
        z_ref[i] = both


def soft(scores):
    top = jnp.max(scores, axis=-1, keepdims=True)
    weights = jnp.exp2((scores - top) * (0.125 * LOG2E))
    total = jnp.sum(weights, axis=-1, keepdims=True)
    return weights.astype(BF16), total, top * 0.125 + jnp.log(total)


def merge(out_a, lse_a, out_b, lse_b):
    top = jnp.maximum(lse_a, lse_b)
    wa, wb = jnp.exp(lse_a - top), jnp.exp(lse_b - top)
    total = wa + wb
    return (wa * out_a + wb * out_b) / total, top + jnp.log(total)


def segment_kernel(y_ref, out_ref):
    n, _, _ = y_ref.shape
    qk = y_ref[:, :32, :].reshape(n * 32, 128).astype(F32)
    low = lane_is_low(qk.shape)
    query = jnp.where(low, qk, 0.0).astype(BF16)
    key = swap(qk).astype(BF16)
    val = y_ref[:, 32:, :].astype(F32).reshape(n * 16, 128)
    other = swap(val).reshape(n, 16, 128)
    val = jnp.concatenate([val.reshape(n, 16, 128), other], axis=1).reshape(n * 32, 128).astype(BF16)
    scores = lax.dot_general(query, key, NT, preferred_element_type=F32)
    probs, total, lse = soft(scores)
    out = jnp.dot(probs, val, preferred_element_type=F32) / total
    out_ref[...] = jnp.where(low, out, lse).reshape(n, 32, 128)


def sequence_kernel(y_ref, z_ref, o_ref, ret_ref):
    n = y_ref.shape[0]
    q2 = jnp.concatenate([y_ref[:, 16 * i : 16 * i + 16, :].astype(F32)[:, 0, :] for i in range(2)], axis=0)
    q2 = jnp.where(lane_is_low(q2.shape), q2, 0.0).astype(BF16)
    kv = z_ref[...].reshape(-1, 128)
    scores = lax.dot_general(q2, kv, NT, preferred_element_type=F32)
    probs, total, lse = soft(scores)
    out = swap(jnp.dot(probs, kv, preferred_element_type=F32) / total)
    row = lax.broadcasted_iota(jnp.int32, (n, 16, 128), 1)
    halves = []
    for i in range(2):
        old = o_ref[:, 16 * i : 16 * i + 16, :]
        first = old[:, 0, :]
        part = slice(n * i, n * i + n)
        mixed, lse_new = merge(first, swap(first), out[part], lse[part])
        first = jnp.where(lane_is_low(first.shape), mixed, swap(lse_new))
        halves.append(jnp.where(row == 0, first[:, None, :], old))
    block = jnp.concatenate(halves, axis=1)
    high, mid, tail = split(block)
    lane = lax.broadcasted_iota(jnp.int32, block.shape, 2)
    last = jnp.where(lane == LSE_LANE, high, jnp.where(lane == LSE_LANE + 1, mid, tail))
    send = jnp.where(lane < 64, high, jnp.where(lane < LSE_LANE, swap(mid), last))
    ret_ref[...] = send.astype(BF16)


def split(x):
    def leading(y):
        scaled = y * 65537.0
        return scaled - (scaled - y)

    high = leading(x)
    rest = x - high
    mid = leading(rest)
    return high, mid, rest - mid


def local_kernel(start, q_hbm, k_hbm, v_hbm, *rest):
    o_ref, buf, sem, out_scr, lse_scr = rest[-5:]
    step, steps = pl.program_id(0), pl.num_programs(0)
    rows = q_hbm.shape[0]
    groups = rows // 16

    def copies(pair):
        lanes, slot = pl.ds(pl.multiple_of((start + pair) * 128, 128), 128), lax.rem(pair, 2)
        return [
            pltpu.make_async_copy(hbm.at[:, lanes], buf.at[slot, i], sem.at[slot, i])
            for i, hbm in enumerate((q_hbm, k_hbm, v_hbm))
        ]

    @pl.when(step == 0)
    def _():
        for copy in copies(step):
            copy.start()

    @pl.when(step + 1 < steps)
    def _():
        for copy in copies(step + 1):
            copy.start()

    for copy in copies(step):
        copy.wait()
    slot = lax.rem(step, 2)
    k, v = buf[slot, 1], buf[slot, 2]
    tall = rows // 2
    low = lane_is_low((tall, 128))
    parts = [slice(i * tall, i * tall + tall) for i in range(2)]
    scores = {}
    for i, part in enumerate(parts):
        q = buf[slot, 0, part, :]
        for half in range(2):
            query = jnp.where(low == (half == 0), q, jnp.zeros_like(q))
            scores[i, half] = lax.dot_general(query, k, NT, preferred_element_type=F32)
    for i, part in enumerate(parts):
        outs, lses = [], []
        for half in range(2):
            probs, total, lse = soft(scores[i, half])
            outs.append(jnp.dot(probs, v, preferred_element_type=F32) / total)
            lses.append(lse)
        out = jnp.where(low, outs[0], outs[1])
        out_scr[part, :] = out
        lse_scr[part, :] = jnp.where(low, lses[0], lses[1])
        o_ref[part, :] = out.astype(BF16)
    lowr = lane_is_low((groups, 128))
    even = pl.ds(2 * (start + step), groups, stride=16)
    odd = pl.ds(2 * (start + step) + 1, groups, stride=16)
    at = rows
    for scr in (out_scr, lse_scr):
        for piece in split(jnp.where(lowr, scr[even, :], scr[odd, :])):
            o_ref[at : at + groups, :] = piece.astype(BF16)
            at += groups


def finish_kernel(period, n_row, local, r_ref, w_ref, out_hbm, buf, out_sem):
    rows, width = out_hbm.shape
    groups = rows // period
    n = r_ref.shape[0]
    low = lane_is_low((groups, 128))
    backs = [r_ref[slot_of(head, n_row, n)] for head in range(HEADS)]
    source = lax.broadcasted_iota(jnp.int32, (128, 128), 0)
    lse_all = jnp.dot(
        jnp.concatenate(backs, axis=0), (source >= LSE_LANE).astype(BF16), preferred_element_type=F32
    )
    has_low = lax.broadcasted_iota(jnp.int32, (groups, 128), 1) < LSE_LANE - 64
    remote = []
    for pair in range(HEADS // 2):
        outs = [backs[2 * pair + half].astype(F32) for half in range(2)]
        outs = [o + jnp.where(has_low, swap(o), 0.0) for o in outs]
        at = 2 * pair * groups
        lse = [lse_all[at + half * groups : at + (half + 1) * groups] for half in range(2)]
        remote.append((jnp.where(low, outs[0], swap(outs[1])), jnp.where(low, lse[0], lse[1])))
    blocks = []
    for pair in range(HEADS // 2):
        lanes = slice(pair * 128, pair * 128 + 128)
        pieces = [
            local[rows + i * groups : rows + (i + 1) * groups, lanes].astype(F32) for i in range(6)
        ]
        out_a, lse_a = (pieces[i] + pieces[i + 1] + pieces[i + 2] for i in (0, 3))
        blocks.append(merge(out_a, lse_a, *remote[pair])[0])
    merged = jnp.concatenate(blocks, axis=1)
    keep = chosen_lanes(period, width)[None]
    own = local[:rows, :].astype(F32).reshape(groups, period, width)
    mixed = jnp.where(keep, merged[:, None, :], own).reshape(rows, width).astype(BF16)
    chunks = buf.shape[0]
    wide = width // chunks
    copies = []
    for c in range(chunks):
        part = pl.ds(c * wide, wide)
        buf[c] = jnp.dot(mixed, w_ref[:, part], preferred_element_type=F32).astype(BF16)
        copy = pltpu.make_async_copy(buf.at[c], out_hbm.at[:, part], out_sem.at[c])
        copy.start()
        copies.append(copy)
    for copy in copies:
        copy.wait()


def shards(queries, keys, values, out_weight):
    n_row, n_col = lax.axis_size("row"), lax.axis_size("col")
    rows, width = queries.shape
    groups = rows // n_col
    shape = jax.ShapeDtypeStruct

    def call(kernel, out, mib=16, **kw):
        params = pltpu.CompilerParams(vmem_limit_bytes=mib * 1024 * 1024)
        return pl.pallas_call(kernel, out_shape=out, compiler_params=params, **kw)

    anywhere = pl.BlockSpec(memory_space=pl.ANY)
    distant = pl.BlockSpec(memory_space=pltpu.HBM)
    whole = pl.BlockSpec(memory_space=pltpu.VMEM)
    packed = call(
        lambda *refs: pack_kernel(n_col, n_row, *refs),
        shape((n_col, groups * 3 // 2, 128), BF16),
        mib=56,
        in_specs=[distant] * 3,
        scratch_shapes=[pltpu.VMEM((3, rows, width), BF16), pltpu.SemaphoreType.DMA((3,))],
    )(queries, keys, values)
    def local(start, count, inputs, aliases):
        pairs = rows * rows * 2 * count
        return call(
            lambda *refs: local_kernel(start, *refs),
            shape((rows + 6 * groups, width), BF16),
            mib=54,
            grid=(count,),
            in_specs=[distant] * 3 + [anywhere] * (len(inputs) - 3),
            out_specs=pl.BlockSpec((rows + 6 * groups, 128), lambda i: (0, start + i)),
            scratch_shapes=[
                pltpu.VMEM((2, 3, rows, 128), BF16),
                pltpu.SemaphoreType.DMA((2, 3)),
                pltpu.VMEM((rows, 128), F32),
                pltpu.VMEM((rows, 128), F32),
            ],
            input_output_aliases=aliases,
            cost_estimate=pl.CostEstimate(
                flops=pairs * 1024, bytes_accessed=count * rows * 128 * 10, transcendentals=pairs
            ),
        )(*inputs)

    inputs = (queries, keys, values)
    packed, *inputs = lax.optimization_barrier((packed, *inputs))
    mine = lax.all_to_all(packed, "col", 0, 0)
    early = HEADS // 3
    first = local(0, early, inputs, {})
    mine, first = lax.optimization_barrier((mine, first))
    top_own = call(middle_kernel, shape((n_row, 2 * n_col, 128), BF16))(mine)
    top_own, mine, first, *inputs = lax.optimization_barrier((top_own, mine, first, *inputs))
    side = int(n_col**0.5)
    owners = [
        [r * n_col + (c if 2 * r < n_row else (side - 1 - c // side) * side + c % side) for r in range(n_row)]
        for c in range(n_col)
    ]
    top_all = lax.all_to_all(top_own, ("row", "col"), 0, 0, axis_index_groups=owners)
    second = local(early, HEADS // 2 - early, (*inputs, first), {3: 0})
    mine, second = lax.optimization_barrier((mine, second))
    segment = call(segment_kernel, shape((n_col, groups, 128), F32))(mine)
    top_all, segment = lax.optimization_barrier((top_all, segment))
    ret = call(
        sequence_kernel,
        shape((n_col, groups, 128), BF16),
        cost_estimate=pl.CostEstimate(flops=10**10, bytes_accessed=10**6, transcendentals=0),
    )(mine, top_all, segment)
    back = lax.all_to_all(ret, "col", 0, 0)
    return call(
        lambda *refs: finish_kernel(n_col, n_row, *refs),
        shape((rows, width), BF16),
        in_specs=[whole] * 3,
        out_specs=anywhere,
        scratch_shapes=[pltpu.VMEM((3, rows, width // 3), BF16), pltpu.SemaphoreType.DMA((3,))],
    )(second, back, out_weight)


def solution(mesh):
    placed = (P(("row", "col"), None), P(("row", "col"), None), P(("row", "col"), None), P())
    return jax.shard_map(
        shards, mesh=mesh, in_specs=placed, out_specs=P(("row", "col"), None), check_vma=False
    )
```

```python
import jax
import jax.numpy as jnp
from jax import lax
from jax.experimental import pallas as pl
from jax.experimental.pallas import tpu as pltpu
from jax.sharding import PartitionSpec as P

HEADS = 12
LOG2E = 1.4426950408889634
LSE_LANE = 125
F32 = jnp.float32
BF16 = jnp.bfloat16
NT = (((1,), (1,)), ((), ()))


def lane_is_low(shape):
    return lax.broadcasted_iota(jnp.int32, shape, len(shape) - 1) < 64


def swap(block):
    return pltpu.roll(block, 64, block.ndim - 1)


def chosen_lanes(period, width):
    offset = lax.broadcasted_iota(jnp.int32, (period, width), 0)
    head = lax.broadcasted_iota(jnp.int32, (period, width), 1) // 64
    return offset == head


LOWER = (0, 3, 1, 2)
UPPER = (3, 0, 2, 1)


def slot_of(head, n_row, n_col):
    side = int(n_col**0.5)
    low, high = LOWER[head // side], UPPER[head // side]
    upper = lax.div(lax.axis_index("row"), n_row // 2)
    return (low + upper * (high - low)) * side + head % side


def owner_groups(n_row, n_col):
    side = int(n_col**0.5)
    half = n_row // 2
    groups = []
    for low, high in zip(LOWER[:-1], UPPER[:-1]):
        for y in range(side):
            groups.append([r * n_col + (low if r < half else high) * side + y for r in range(n_row)])
    for rows, z in ((range(half), LOWER[-1]), (range(half, n_row), UPPER[-1])):
        for y in range(0, side, 2):
            groups.append([r * n_col + z * side + y + i for i in range(2) for r in rows])
    return groups


def pack_kernel(period, n_row, q_hbm, k_hbm, v_hbm, x_ref, buf, sem):
    rows, width = q_hbm.shape
    copies = [
        pltpu.make_async_copy(hbm, buf.at[i], sem.at[i])
        for i, hbm in enumerate((q_hbm, k_hbm, v_hbm))
    ]
    for copy in copies:
        copy.start()
    groups = rows // period
    keep = chosen_lanes(period, width).astype(BF16)
    member = (
        lax.broadcasted_iota(jnp.int32, (groups, rows), 1) // period
        == lax.broadcasted_iota(jnp.int32, (groups, rows), 0)
    ).astype(BF16)

    def pick(i):
        copies[i].wait()
        kept = buf[i].reshape(groups, period, width) * keep[None]
        return jnp.dot(member, kept.reshape(rows, width), preferred_element_type=F32)

    q, k = pick(0), pick(1)
    low = lane_is_low((groups, 128))
    low_half = lane_is_low((groups // 2, 128))
    pairs = [
        (slice(i * 128, i * 128 + 128), slot_of(2 * i, n_row, period), slot_of(2 * i + 1, n_row, period))
        for i in range(HEADS // 2)
    ]
    for lanes, even, odd in pairs:
        qb, kb = q[:, lanes], k[:, lanes]
        x_ref[even, :groups] = jnp.where(low, qb, swap(kb)).astype(BF16)
        x_ref[odd, :groups] = jnp.where(low, swap(qb), kb).astype(BF16)
    v = pick(2)
    for lanes, even, odd in pairs:
        top, bottom = v[: groups // 2, lanes], v[groups // 2 :, lanes]
        x_ref[even, groups:] = jnp.where(low_half, top, swap(bottom)).astype(BF16)
        x_ref[odd, groups:] = jnp.where(low_half, swap(top), bottom).astype(BF16)
    for rest in range(HEADS, x_ref.shape[0]):
        x_ref[slot_of(rest, n_row, period)] = jnp.zeros(x_ref.shape[1:], BF16)


def middle_kernel(y_ref, z_ref):
    y = y_ref[...].astype(F32)
    first, second, val = y[:, 0, :], y[:, 16, :], y[:, 32, :]
    low = lane_is_low(first.shape)
    top = jnp.where(low, swap(first), swap(val)).astype(BF16)
    bottom = jnp.where(low, swap(second), val).astype(BF16)
    both = jnp.concatenate([top, bottom], axis=0)
    for i in range(z_ref.shape[0]):
        z_ref[i] = both


def soft(scores):
    top = jnp.max(scores, axis=-1, keepdims=True)
    weights = jnp.exp2((scores - top) * (0.125 * LOG2E))
    total = jnp.sum(weights, axis=-1, keepdims=True)
    return weights.astype(BF16), total, top * 0.125 + jnp.log(total)


def merge(out_a, lse_a, out_b, lse_b):
    top = jnp.maximum(lse_a, lse_b)
    wa, wb = jnp.exp(lse_a - top), jnp.exp(lse_b - top)
    total = wa + wb
    return (wa * out_a + wb * out_b) / total, top + jnp.log(total)


def segment_kernel(y_ref, out_ref):
    n, _, _ = y_ref.shape
    qk = y_ref[:, :32, :].reshape(n * 32, 128).astype(F32)
    low = lane_is_low(qk.shape)
    query = jnp.where(low, qk, 0.0).astype(BF16)
    key = swap(qk).astype(BF16)
    val = y_ref[:, 32:, :].astype(F32).reshape(n * 16, 128)
    other = swap(val).reshape(n, 16, 128)
    val = jnp.concatenate([val.reshape(n, 16, 128), other], axis=1).reshape(n * 32, 128).astype(BF16)
    scores = lax.dot_general(query, key, NT, preferred_element_type=F32)
    probs, total, lse = soft(scores)
    out = jnp.dot(probs, val, preferred_element_type=F32) / total
    out_ref[...] = jnp.where(low, out, lse).reshape(n, 32, 128)


def sequence_kernel(y_ref, z_ref, o_ref, ret_ref):
    n = y_ref.shape[0]
    q2 = jnp.concatenate([y_ref[:, 16 * i : 16 * i + 16, :].astype(F32)[:, 0, :] for i in range(2)], axis=0)
    q2 = jnp.where(lane_is_low(q2.shape), q2, 0.0).astype(BF16)
    kv = z_ref[...].reshape(-1, 128)
    scores = lax.dot_general(q2, kv, NT, preferred_element_type=F32)
    probs, total, lse = soft(scores)
    out = swap(jnp.dot(probs, kv, preferred_element_type=F32) / total)
    row = lax.broadcasted_iota(jnp.int32, (n, 16, 128), 1)
    halves = []
    for i in range(2):
        old = o_ref[:, 16 * i : 16 * i + 16, :]
        first = old[:, 0, :]
        part = slice(n * i, n * i + n)
        mixed, lse_new = merge(first, swap(first), out[part], lse[part])
        first = jnp.where(lane_is_low(first.shape), mixed, swap(lse_new))
        halves.append(jnp.where(row == 0, first[:, None, :], old))
    block = jnp.concatenate(halves, axis=1)
    high, mid, tail = split(block)
    lane = lax.broadcasted_iota(jnp.int32, block.shape, 2)
    last = jnp.where(lane == LSE_LANE, high, jnp.where(lane == LSE_LANE + 1, mid, tail))
    send = jnp.where(lane < 64, high, jnp.where(lane < LSE_LANE, swap(mid), last))
    ret_ref[...] = send.astype(BF16)


def split(x):
    def leading(y):
        scaled = y * 65537.0
        return scaled - (scaled - y)

    high = leading(x)
    rest = x - high
    mid = leading(rest)
    return high, mid, rest - mid


def local_kernel(start, q_hbm, k_hbm, v_hbm, *rest):
    o_ref, buf, sem, out_scr, lse_scr = rest[-5:]
    step, steps = pl.program_id(0), pl.num_programs(0)
    rows = q_hbm.shape[0]
    groups = rows // 16

    def copies(pair):
        lanes, slot = pl.ds(pl.multiple_of((start + pair) * 128, 128), 128), lax.rem(pair, 2)
        return [
            pltpu.make_async_copy(hbm.at[:, lanes], buf.at[slot, i], sem.at[slot, i])
            for i, hbm in enumerate((q_hbm, k_hbm, v_hbm))
        ]

    @pl.when(step == 0)
    def _():
        for copy in copies(step):
            copy.start()

    @pl.when(step + 1 < steps)
    def _():
        for copy in copies(step + 1):
            copy.start()

    for copy in copies(step):
        copy.wait()
    slot = lax.rem(step, 2)
    k, v = buf[slot, 1], buf[slot, 2]
    tall = rows // 2
    low = lane_is_low((tall, 128))
    parts = [slice(i * tall, i * tall + tall) for i in range(2)]
    scores = {}
    for i, part in enumerate(parts):
        q = buf[slot, 0, part, :]
        for half in range(2):
            query = jnp.where(low == (half == 0), q, jnp.zeros_like(q))
            scores[i, half] = lax.dot_general(query, k, NT, preferred_element_type=F32)
    for i, part in enumerate(parts):
        outs, lses = [], []
        for half in range(2):
            probs, total, lse = soft(scores[i, half])
            outs.append(jnp.dot(probs, v, preferred_element_type=F32) / total)
            lses.append(lse)
        out = jnp.where(low, outs[0], outs[1])
        out_scr[part, :] = out
        lse_scr[part, :] = jnp.where(low, lses[0], lses[1])
        o_ref[part, :] = out.astype(BF16)
    lowr = lane_is_low((groups, 128))
    even = pl.ds(2 * (start + step), groups, stride=16)
    odd = pl.ds(2 * (start + step) + 1, groups, stride=16)
    at = rows
    for scr in (out_scr, lse_scr):
        for piece in split(jnp.where(lowr, scr[even, :], scr[odd, :])):
            o_ref[at : at + groups, :] = piece.astype(BF16)
            at += groups


def finish_kernel(period, n_row, local, r_ref, w_ref, out_hbm, buf, out_sem):
    rows, width = out_hbm.shape
    groups = rows // period
    n = r_ref.shape[0]
    low = lane_is_low((groups, 128))
    backs = [r_ref[slot_of(head, n_row, n)] for head in range(HEADS)]
    source = lax.broadcasted_iota(jnp.int32, (128, 128), 0)
    lse_all = jnp.dot(
        jnp.concatenate(backs, axis=0), (source >= LSE_LANE).astype(BF16), preferred_element_type=F32
    )
    has_low = lax.broadcasted_iota(jnp.int32, (groups, 128), 1) < LSE_LANE - 64
    remote = []
    for pair in range(HEADS // 2):
        outs = [backs[2 * pair + half].astype(F32) for half in range(2)]
        outs = [o + jnp.where(has_low, swap(o), 0.0) for o in outs]
        at = 2 * pair * groups
        lse = [lse_all[at + half * groups : at + (half + 1) * groups] for half in range(2)]
        remote.append((jnp.where(low, outs[0], swap(outs[1])), jnp.where(low, lse[0], lse[1])))
    blocks = []
    for pair in range(HEADS // 2):
        lanes = slice(pair * 128, pair * 128 + 128)
        pieces = [
            local[rows + i * groups : rows + (i + 1) * groups, lanes].astype(F32) for i in range(6)
        ]
        out_a, lse_a = (pieces[i] + pieces[i + 1] + pieces[i + 2] for i in (0, 3))
        blocks.append(merge(out_a, lse_a, *remote[pair])[0])
    merged = jnp.concatenate(blocks, axis=1)
    keep = chosen_lanes(period, width)[None]
    chunks = buf.shape[0]
    tall, wide = rows // chunks, groups // chunks
    copies = []
    for c in range(chunks):
        part = slice(c * tall, c * tall + tall)
        own = local[part, :].astype(F32).reshape(wide, period, width)
        mixed = jnp.where(keep, merged[c * wide : c * wide + wide][:, None, :], own)
        mixed = mixed.reshape(tall, width).astype(BF16)
        buf[c] = jnp.dot(mixed, w_ref[...], preferred_element_type=F32).astype(BF16)
        copy = pltpu.make_async_copy(buf.at[c], out_hbm.at[pl.ds(c * tall, tall)], out_sem.at[c])
        copy.start()
        copies.append(copy)
    for copy in copies:
        copy.wait()


def shards(queries, keys, values, out_weight):
    n_row, n_col = lax.axis_size("row"), lax.axis_size("col")
    rows, width = queries.shape
    groups = rows // n_col
    shape = jax.ShapeDtypeStruct

    def call(kernel, out, mib=16, **kw):
        params = pltpu.CompilerParams(vmem_limit_bytes=mib * 1024 * 1024)
        return pl.pallas_call(kernel, out_shape=out, compiler_params=params, **kw)

    anywhere = pl.BlockSpec(memory_space=pl.ANY)
    distant = pl.BlockSpec(memory_space=pltpu.HBM)
    whole = pl.BlockSpec(memory_space=pltpu.VMEM)
    packed = call(
        lambda *refs: pack_kernel(n_col, n_row, *refs),
        shape((n_col, groups * 3 // 2, 128), BF16),
        mib=56,
        in_specs=[distant] * 3,
        scratch_shapes=[pltpu.VMEM((3, rows, width), BF16), pltpu.SemaphoreType.DMA((3,))],
    )(queries, keys, values)
    def local(start, count, inputs, aliases):
        pairs = rows * rows * 2 * count
        return call(
            lambda *refs: local_kernel(start, *refs),
            shape((rows + 6 * groups, width), BF16),
            mib=54,
            grid=(count,),
            in_specs=[distant] * 3 + [anywhere] * (len(inputs) - 3),
            out_specs=pl.BlockSpec((rows + 6 * groups, 128), lambda i: (0, start + i)),
            scratch_shapes=[
                pltpu.VMEM((2, 3, rows, 128), BF16),
                pltpu.SemaphoreType.DMA((2, 3)),
                pltpu.VMEM((rows, 128), F32),
                pltpu.VMEM((rows, 128), F32),
            ],
            input_output_aliases=aliases,
            cost_estimate=pl.CostEstimate(
                flops=pairs * 1024, bytes_accessed=count * rows * 128 * 10, transcendentals=pairs
            ),
        )(*inputs)

    inputs = (queries, keys, values)
    packed, *inputs = lax.optimization_barrier((packed, *inputs))
    mine = lax.all_to_all(packed, "col", 0, 0)
    early = HEADS // 3
    first = local(0, early, inputs, {})
    mine, first = lax.optimization_barrier((mine, first))
    top_own = call(middle_kernel, shape((n_row, 2 * n_col, 128), BF16))(mine)
    top_own, mine, first, *inputs = lax.optimization_barrier((top_own, mine, first, *inputs))
    owners = owner_groups(n_row, n_col)
    top_all = lax.all_to_all(top_own, ("row", "col"), 0, 0, axis_index_groups=owners)
    second = local(early, HEADS // 2 - early, (*inputs, first), {3: 0})
    mine, second = lax.optimization_barrier((mine, second))
    segment = call(segment_kernel, shape((n_col, groups, 128), F32))(mine)
    top_all, segment = lax.optimization_barrier((top_all, segment))
    ret = call(
        sequence_kernel,
        shape((n_col, groups, 128), BF16),
        cost_estimate=pl.CostEstimate(flops=10**10, bytes_accessed=10**6, transcendentals=0),
    )(mine, top_all, segment)
    back = lax.all_to_all(ret, "col", 0, 0)
    return call(
        lambda *refs: finish_kernel(n_col, n_row, *refs),
        shape((rows, width), BF16),
        in_specs=[whole] * 3,
        out_specs=anywhere,
        scratch_shapes=[pltpu.VMEM((4, rows // 4, width), BF16), pltpu.SemaphoreType.DMA((4,))],
    )(second, back, out_weight)


def solution(mesh):
    placed = (P(("row", "col"), None), P(("row", "col"), None), P(("row", "col"), None), P())
    return jax.shard_map(
        shards, mesh=mesh, in_specs=placed, out_specs=P(("row", "col"), None), check_vma=False
    )
```

```python
import jax
import jax.numpy as jnp
from jax import lax
from jax.experimental import pallas as pl
from jax.experimental.pallas import tpu as pltpu
from jax.sharding import PartitionSpec as P

HEADS = 12
LOG2E = 1.4426950408889634
LSE_LANE = 125
F32 = jnp.float32
BF16 = jnp.bfloat16
NT = (((1,), (1,)), ((), ()))


def lane_is_low(shape):
    return lax.broadcasted_iota(jnp.int32, shape, len(shape) - 1) < 64


def swap(block):
    return pltpu.roll(block, 64, block.ndim - 1)


def chosen_lanes(period, width):
    offset = lax.broadcasted_iota(jnp.int32, (period, width), 0)
    head = lax.broadcasted_iota(jnp.int32, (period, width), 1) // 64
    return offset == head


LOWER = (0, 3, 1, 2)
UPPER = (3, 0, 2, 1)


ORDER = (1, 0, 2, 3)


def col_order(n_col):
    side = int(n_col**0.5)
    return [[z * side + y for z in ORDER for y in range(side)]]


def slot_of(head, n_row, n_col):
    side = int(n_col**0.5)
    low, high = ORDER.index(LOWER[head // side]), ORDER.index(UPPER[head // side])
    upper = lax.div(lax.axis_index("row"), n_row // 2)
    return (low + upper * (high - low)) * side + head % side


def owner_groups(n_row, n_col):
    side = int(n_col**0.5)
    half = n_row // 2
    groups = []
    for low, high in zip(LOWER[:-1], UPPER[:-1]):
        for y in range(side):
            groups.append([r * n_col + (low if r < half else high) * side + y for r in range(n_row)])
    for rows, z in ((range(half), LOWER[-1]), (range(half, n_row), UPPER[-1])):
        for y in range(0, side, 2):
            groups.append([r * n_col + z * side + y + i for i in range(2) for r in rows])
    return groups


def pack_kernel(period, n_row, q_hbm, k_hbm, v_hbm, x_hbm, buf, sem, x_ref, out_sem):
    rows, width = q_hbm.shape
    copies = [
        pltpu.make_async_copy(hbm, buf.at[i], sem.at[i])
        for i, hbm in enumerate((q_hbm, k_hbm, v_hbm))
    ]
    for copy in copies:
        copy.start()
    groups = rows // period
    ends = (pl.ds(0, groups), pl.ds(groups, groups // 2))
    sends = [
        pltpu.make_async_copy(x_ref.at[:, part], x_hbm.at[:, part], out_sem.at[i])
        for i, part in enumerate(ends)
    ]
    for rest in range(HEADS, x_ref.shape[0]):
        x_ref[slot_of(rest, n_row, period)] = jnp.zeros(x_ref.shape[1:], BF16)
    keep = chosen_lanes(period, width).astype(BF16)
    member = (
        lax.broadcasted_iota(jnp.int32, (groups, rows), 1) // period
        == lax.broadcasted_iota(jnp.int32, (groups, rows), 0)
    ).astype(BF16)

    def pick(i):
        copies[i].wait()
        kept = buf[i].reshape(groups, period, width) * keep[None]
        return jnp.dot(member, kept.reshape(rows, width), preferred_element_type=F32)

    q, k = pick(0), pick(1)
    low = lane_is_low((groups, 128))
    low_half = lane_is_low((groups // 2, 128))
    pairs = [
        (slice(i * 128, i * 128 + 128), slot_of(2 * i, n_row, period), slot_of(2 * i + 1, n_row, period))
        for i in range(HEADS // 2)
    ]
    for lanes, even, odd in pairs:
        qb, kb = q[:, lanes], k[:, lanes]
        x_ref[even, :groups] = jnp.where(low, qb, swap(kb)).astype(BF16)
        x_ref[odd, :groups] = jnp.where(low, swap(qb), kb).astype(BF16)
    sends[0].start()
    v = pick(2)
    for lanes, even, odd in pairs:
        top, bottom = v[: groups // 2, lanes], v[groups // 2 :, lanes]
        x_ref[even, groups:] = jnp.where(low_half, top, swap(bottom)).astype(BF16)
        x_ref[odd, groups:] = jnp.where(low_half, swap(top), bottom).astype(BF16)
    sends[1].start()
    for send in sends:
        send.wait()


def middle_kernel(y_ref, z_ref):
    y = y_ref[...].astype(F32)
    first, second, val = y[:, 0, :], y[:, 16, :], y[:, 32, :]
    low = lane_is_low(first.shape)
    top = jnp.where(low, swap(first), swap(val)).astype(BF16)
    bottom = jnp.where(low, swap(second), val).astype(BF16)
    both = jnp.concatenate([top, bottom], axis=0)
    for i in range(z_ref.shape[0]):
        z_ref[i] = both


def soft(scores):
    top = jnp.max(scores, axis=-1, keepdims=True)
    weights = jnp.exp2((scores - top) * (0.125 * LOG2E))
    total = jnp.sum(weights, axis=-1, keepdims=True)
    return weights.astype(BF16), total, top * 0.125 + jnp.log(total)


def merge(out_a, lse_a, out_b, lse_b):
    top = jnp.maximum(lse_a, lse_b)
    wa, wb = jnp.exp(lse_a - top), jnp.exp(lse_b - top)
    total = wa + wb
    return (wa * out_a + wb * out_b) / total, top + jnp.log(total)


def segment_kernel(y_ref, out_ref):
    n, _, _ = y_ref.shape
    qk = y_ref[:, :32, :].reshape(n * 32, 128).astype(F32)
    low = lane_is_low(qk.shape)
    query = jnp.where(low, qk, 0.0).astype(BF16)
    key = swap(qk).astype(BF16)
    val = y_ref[:, 32:, :].astype(F32).reshape(n * 16, 128)
    other = swap(val).reshape(n, 16, 128)
    val = jnp.concatenate([val.reshape(n, 16, 128), other], axis=1).reshape(n * 32, 128).astype(BF16)
    scores = lax.dot_general(query, key, NT, preferred_element_type=F32)
    probs, total, lse = soft(scores)
    out = jnp.dot(probs, val, preferred_element_type=F32) / total
    out_ref[...] = jnp.where(low, out, lse).reshape(n, 32, 128)


def sequence_kernel(y_ref, z_ref, o_ref, ret_ref):
    n = y_ref.shape[0]
    q2 = jnp.concatenate([y_ref[:, 16 * i : 16 * i + 16, :].astype(F32)[:, 0, :] for i in range(2)], axis=0)
    q2 = jnp.where(lane_is_low(q2.shape), q2, 0.0).astype(BF16)
    kv = z_ref[...].reshape(-1, 128)
    scores = lax.dot_general(q2, kv, NT, preferred_element_type=F32)
    probs, total, lse = soft(scores)
    out = swap(jnp.dot(probs, kv, preferred_element_type=F32) / total)
    row = lax.broadcasted_iota(jnp.int32, (n, 16, 128), 1)
    halves = []
    for i in range(2):
        old = o_ref[:, 16 * i : 16 * i + 16, :]
        first = old[:, 0, :]
        part = slice(n * i, n * i + n)
        mixed, lse_new = merge(first, swap(first), out[part], lse[part])
        first = jnp.where(lane_is_low(first.shape), mixed, swap(lse_new))
        halves.append(jnp.where(row == 0, first[:, None, :], old))
    block = jnp.concatenate(halves, axis=1)
    high, mid, tail = split(block)
    lane = lax.broadcasted_iota(jnp.int32, block.shape, 2)
    last = jnp.where(lane == LSE_LANE, high, jnp.where(lane == LSE_LANE + 1, mid, tail))
    send = jnp.where(lane < 64, high, jnp.where(lane < LSE_LANE, swap(mid), last))
    ret_ref[...] = send.astype(BF16)


def split(x):
    def leading(y):
        scaled = y * 65537.0
        return scaled - (scaled - y)

    high = leading(x)
    rest = x - high
    mid = leading(rest)
    return high, mid, rest - mid


def local_kernel(start, q_hbm, k_hbm, v_hbm, *rest):
    o_ref, buf, sem, out_scr, lse_scr = rest[-5:]
    step, steps = pl.program_id(0), pl.num_programs(0)
    rows = q_hbm.shape[0]
    groups = rows // 16

    def copies(pair):
        lanes, slot = pl.ds(pl.multiple_of((start + pair) * 128, 128), 128), lax.rem(pair, 2)
        return [
            pltpu.make_async_copy(hbm.at[:, lanes], buf.at[slot, i], sem.at[slot, i])
            for i, hbm in enumerate((q_hbm, k_hbm, v_hbm))
        ]

    @pl.when(step == 0)
    def _():
        for copy in copies(step):
            copy.start()

    @pl.when(step + 1 < steps)
    def _():
        for copy in copies(step + 1):
            copy.start()

    for copy in copies(step):
        copy.wait()
    slot = lax.rem(step, 2)
    k, v = buf[slot, 1], buf[slot, 2]
    tall = rows // 2
    low = lane_is_low((tall, 128))
    parts = [slice(i * tall, i * tall + tall) for i in range(2)]
    scores = {}
    for i, part in enumerate(parts):
        q = buf[slot, 0, part, :]
        for half in range(2):
            query = jnp.where(low == (half == 0), q, jnp.zeros_like(q))
            scores[i, half] = lax.dot_general(query, k, NT, preferred_element_type=F32)
    for i, part in enumerate(parts):
        outs, lses = [], []
        for half in range(2):
            probs, total, lse = soft(scores[i, half])
            outs.append(jnp.dot(probs, v, preferred_element_type=F32) / total)
            lses.append(lse)
        out = jnp.where(low, outs[0], outs[1])
        out_scr[part, :] = out
        lse_scr[part, :] = jnp.where(low, lses[0], lses[1])
        o_ref[part, :] = out.astype(BF16)
    lowr = lane_is_low((groups, 128))
    even = pl.ds(2 * (start + step), groups, stride=16)
    odd = pl.ds(2 * (start + step) + 1, groups, stride=16)
    at = rows
    for scr in (out_scr, lse_scr):
        for piece in split(jnp.where(lowr, scr[even, :], scr[odd, :])):
            o_ref[at : at + groups, :] = piece.astype(BF16)
            at += groups


def finish_kernel(period, n_row, local, r_ref, w_ref, out_hbm, buf, out_sem):
    rows, width = out_hbm.shape
    groups = rows // period
    n = r_ref.shape[0]
    low = lane_is_low((groups, 128))
    backs = [r_ref[slot_of(head, n_row, n)] for head in range(HEADS)]
    source = lax.broadcasted_iota(jnp.int32, (128, 128), 0)
    lse_all = jnp.dot(
        jnp.concatenate(backs, axis=0), (source >= LSE_LANE).astype(BF16), preferred_element_type=F32
    )
    has_low = lax.broadcasted_iota(jnp.int32, (groups, 128), 1) < LSE_LANE - 64
    remote = []
    for pair in range(HEADS // 2):
        outs = [backs[2 * pair + half].astype(F32) for half in range(2)]
        outs = [o + jnp.where(has_low, swap(o), 0.0) for o in outs]
        at = 2 * pair * groups
        lse = [lse_all[at + half * groups : at + (half + 1) * groups] for half in range(2)]
        remote.append((jnp.where(low, outs[0], swap(outs[1])), jnp.where(low, lse[0], lse[1])))
    blocks = []
    for pair in range(HEADS // 2):
        lanes = slice(pair * 128, pair * 128 + 128)
        pieces = [
            local[rows + i * groups : rows + (i + 1) * groups, lanes].astype(F32) for i in range(6)
        ]
        out_a, lse_a = (pieces[i] + pieces[i + 1] + pieces[i + 2] for i in (0, 3))
        blocks.append(merge(out_a, lse_a, *remote[pair])[0])
    merged = jnp.concatenate(blocks, axis=1)
    keep = chosen_lanes(period, width)[None]
    chunks = buf.shape[0]
    tall, wide = rows // chunks, groups // chunks
    copies = []
    for c in range(chunks):
        part = slice(c * tall, c * tall + tall)
        own = local[part, :].astype(F32).reshape(wide, period, width)
        mixed = jnp.where(keep, merged[c * wide : c * wide + wide][:, None, :], own)
        mixed = mixed.reshape(tall, width).astype(BF16)
        buf[c] = jnp.dot(mixed, w_ref[...], preferred_element_type=F32).astype(BF16)
        copy = pltpu.make_async_copy(buf.at[c], out_hbm.at[pl.ds(c * tall, tall)], out_sem.at[c])
        copy.start()
        copies.append(copy)
    for copy in copies:
        copy.wait()


def shards(queries, keys, values, out_weight):
    n_row, n_col = lax.axis_size("row"), lax.axis_size("col")
    rows, width = queries.shape
    groups = rows // n_col
    shape = jax.ShapeDtypeStruct

    def call(kernel, out, mib=16, **kw):
        params = pltpu.CompilerParams(vmem_limit_bytes=mib * 1024 * 1024)
        return pl.pallas_call(kernel, out_shape=out, compiler_params=params, **kw)

    anywhere = pl.BlockSpec(memory_space=pl.ANY)
    distant = pl.BlockSpec(memory_space=pltpu.HBM)
    whole = pl.BlockSpec(memory_space=pltpu.VMEM)
    packed = call(
        lambda *refs: pack_kernel(n_col, n_row, *refs),
        shape((n_col, groups * 3 // 2, 128), BF16),
        mib=56,
        in_specs=[distant] * 3,
        out_specs=anywhere,
        scratch_shapes=[
            pltpu.VMEM((3, rows, width), BF16),
            pltpu.SemaphoreType.DMA((3,)),
            pltpu.VMEM((n_col, groups * 3 // 2, 128), BF16),
            pltpu.SemaphoreType.DMA((2,)),
        ],
    )(queries, keys, values)
    def local(start, count, inputs, aliases):
        pairs = rows * rows * 2 * count
        return call(
            lambda *refs: local_kernel(start, *refs),
            shape((rows + 6 * groups, width), BF16),
            mib=54,
            grid=(count,),
            in_specs=[distant] * 3 + [anywhere] * (len(inputs) - 3),
            out_specs=pl.BlockSpec((rows + 6 * groups, 128), lambda i: (0, start + i)),
            scratch_shapes=[
                pltpu.VMEM((2, 3, rows, 128), BF16),
                pltpu.SemaphoreType.DMA((2, 3)),
                pltpu.VMEM((rows, 128), F32),
                pltpu.VMEM((rows, 128), F32),
            ],
            input_output_aliases=aliases,
            cost_estimate=pl.CostEstimate(
                flops=pairs * 1024, bytes_accessed=count * rows * 128 * 10, transcendentals=pairs
            ),
        )(*inputs)

    inputs = (queries, keys, values)
    packed, *inputs = lax.optimization_barrier((packed, *inputs))
    mine = lax.all_to_all(packed, "col", 0, 0, axis_index_groups=col_order(n_col))
    early = HEADS // 3
    first = local(0, early, inputs, {})
    mine, first = lax.optimization_barrier((mine, first))
    top_own = call(middle_kernel, shape((n_row, 2 * n_col, 128), BF16))(mine)
    top_own, mine, first, *inputs = lax.optimization_barrier((top_own, mine, first, *inputs))
    owners = owner_groups(n_row, n_col)
    top_all = lax.all_to_all(top_own, ("row", "col"), 0, 0, axis_index_groups=owners)
    second = local(early, HEADS // 2 - early, (*inputs, first), {3: 0})
    mine, second = lax.optimization_barrier((mine, second))
    segment = call(segment_kernel, shape((n_col, groups, 128), F32))(mine)
    top_all, segment = lax.optimization_barrier((top_all, segment))
    ret = call(
        sequence_kernel,
        shape((n_col, groups, 128), BF16),
        cost_estimate=pl.CostEstimate(flops=10**10, bytes_accessed=10**6, transcendentals=0),
    )(mine, top_all, segment)
    back = lax.all_to_all(ret, "col", 0, 0, axis_index_groups=col_order(n_col))
    return call(
        lambda *refs: finish_kernel(n_col, n_row, *refs),
        shape((rows, width), BF16),
        in_specs=[whole] * 3,
        out_specs=anywhere,
        scratch_shapes=[pltpu.VMEM((4, rows // 4, width), BF16), pltpu.SemaphoreType.DMA((4,))],
    )(second, back, out_weight)


def solution(mesh):
    placed = (P(("row", "col"), None), P(("row", "col"), None), P(("row", "col"), None), P())
    return jax.shard_map(
        shards, mesh=mesh, in_specs=placed, out_specs=P(("row", "col"), None), check_vma=False
    )
```

```python
import jax
import jax.numpy as jnp
from jax import lax
from jax.experimental import pallas as pl
from jax.experimental.pallas import tpu as pltpu
from jax.sharding import PartitionSpec as P

HEADS = 12
LOG2E = 1.4426950408889634
LSE_LANE = 125
F32 = jnp.float32
BF16 = jnp.bfloat16
NT = (((1,), (1,)), ((), ()))


def lane_is_low(shape):
    return lax.broadcasted_iota(jnp.int32, shape, len(shape) - 1) < 64


def swap(block):
    return pltpu.roll(block, 64, block.ndim - 1)


def chosen_lanes(period, width):
    offset = lax.broadcasted_iota(jnp.int32, (period, width), 0)
    head = lax.broadcasted_iota(jnp.int32, (period, width), 1) // 64
    return offset == head


LOWER = (0, 3, 1, 2)
UPPER = (3, 0, 2, 1)


ORDER = (1, 0, 2, 3)


def col_order(n_col):
    side = int(n_col**0.5)
    return [[z * side + y for z in ORDER for y in range(side)]]


def slot_of(head, n_row, n_col):
    side = int(n_col**0.5)
    low, high = ORDER.index(LOWER[head // side]), ORDER.index(UPPER[head // side])
    upper = lax.div(lax.axis_index("row"), n_row // 2)
    return (low + upper * (high - low)) * side + head % side


def owner_groups(n_row, n_col):
    side = int(n_col**0.5)
    half = n_row // 2
    groups = []
    for low, high in zip(LOWER[:-1], UPPER[:-1]):
        for y in range(side):
            rows = [r ^ 1 for r in range(n_row)]
            groups.append([r * n_col + (low if r < half else high) * side + y for r in rows])
    for rows, z in ((range(half), LOWER[-1]), (range(half, n_row), UPPER[-1])):
        for y in range(0, side, 2):
            groups.append([r * n_col + z * side + y + i for i in range(2) for r in rows])
    return groups


def pack_kernel(period, n_row, q_hbm, k_hbm, v_hbm, x_hbm, buf, sem, x_ref, out_sem):
    rows, width = q_hbm.shape
    copies = [
        pltpu.make_async_copy(hbm, buf.at[i], sem.at[i])
        for i, hbm in enumerate((q_hbm, k_hbm, v_hbm))
    ]
    for copy in copies:
        copy.start()
    groups = rows // period
    ends = (pl.ds(0, groups), pl.ds(groups, groups // 2))
    sends = [
        pltpu.make_async_copy(x_ref.at[:, part], x_hbm.at[:, part], out_sem.at[i])
        for i, part in enumerate(ends)
    ]
    for rest in range(HEADS, x_ref.shape[0]):
        x_ref[slot_of(rest, n_row, period)] = jnp.zeros(x_ref.shape[1:], BF16)
    keep = chosen_lanes(period, width).astype(BF16)
    member = (
        lax.broadcasted_iota(jnp.int32, (groups, rows), 1) // period
        == lax.broadcasted_iota(jnp.int32, (groups, rows), 0)
    ).astype(BF16)

    def pick(i):
        copies[i].wait()
        kept = buf[i].reshape(groups, period, width) * keep[None]
        return jnp.dot(member, kept.reshape(rows, width), preferred_element_type=F32)

    q, k = pick(0), pick(1)
    low = lane_is_low((groups, 128))
    low_half = lane_is_low((groups // 2, 128))
    pairs = [
        (slice(i * 128, i * 128 + 128), slot_of(2 * i, n_row, period), slot_of(2 * i + 1, n_row, period))
        for i in range(HEADS // 2)
    ]
    for lanes, even, odd in pairs:
        qb, kb = q[:, lanes], k[:, lanes]
        x_ref[even, :groups] = jnp.where(low, qb, swap(kb)).astype(BF16)
        x_ref[odd, :groups] = jnp.where(low, swap(qb), kb).astype(BF16)
    sends[0].start()
    v = pick(2)
    for lanes, even, odd in pairs:
        top, bottom = v[: groups // 2, lanes], v[groups // 2 :, lanes]
        x_ref[even, groups:] = jnp.where(low_half, top, swap(bottom)).astype(BF16)
        x_ref[odd, groups:] = jnp.where(low_half, swap(top), bottom).astype(BF16)
    sends[1].start()
    for send in sends:
        send.wait()


def middle_kernel(y_ref, z_ref):
    y = y_ref[...].astype(F32)
    first, second, val = y[:, 0, :], y[:, 16, :], y[:, 32, :]
    low = lane_is_low(first.shape)
    top = jnp.where(low, swap(first), swap(val)).astype(BF16)
    bottom = jnp.where(low, swap(second), val).astype(BF16)
    both = jnp.concatenate([top, bottom], axis=0)
    for i in range(z_ref.shape[0]):
        z_ref[i] = both


def soft(scores):
    top = jnp.max(scores, axis=-1, keepdims=True)
    weights = jnp.exp2((scores - top) * (0.125 * LOG2E))
    total = jnp.sum(weights, axis=-1, keepdims=True)
    return weights.astype(BF16), total, top * 0.125 + jnp.log(total)


def merge(out_a, lse_a, out_b, lse_b):
    top = jnp.maximum(lse_a, lse_b)
    wa, wb = jnp.exp(lse_a - top), jnp.exp(lse_b - top)
    total = wa + wb
    return (wa * out_a + wb * out_b) / total, top + jnp.log(total)


def segment_kernel(y_ref, out_ref):
    n, _, _ = y_ref.shape
    qk = y_ref[:, :32, :].reshape(n * 32, 128).astype(F32)
    low = lane_is_low(qk.shape)
    query = jnp.where(low, qk, 0.0).astype(BF16)
    key = swap(qk).astype(BF16)
    val = y_ref[:, 32:, :].astype(F32).reshape(n * 16, 128)
    other = swap(val).reshape(n, 16, 128)
    val = jnp.concatenate([val.reshape(n, 16, 128), other], axis=1).reshape(n * 32, 128).astype(BF16)
    scores = lax.dot_general(query, key, NT, preferred_element_type=F32)
    probs, total, lse = soft(scores)
    out = jnp.dot(probs, val, preferred_element_type=F32) / total
    out_ref[...] = jnp.where(low, out, lse).reshape(n, 32, 128)


def sequence_kernel(y_ref, z_ref, o_ref, ret_ref):
    n = y_ref.shape[0]
    q2 = jnp.concatenate([y_ref[:, 16 * i : 16 * i + 16, :].astype(F32)[:, 0, :] for i in range(2)], axis=0)
    q2 = jnp.where(lane_is_low(q2.shape), q2, 0.0).astype(BF16)
    kv = z_ref[...].reshape(-1, 128)
    scores = lax.dot_general(q2, kv, NT, preferred_element_type=F32)
    probs, total, lse = soft(scores)
    out = swap(jnp.dot(probs, kv, preferred_element_type=F32) / total)
    row = lax.broadcasted_iota(jnp.int32, (n, 16, 128), 1)
    halves = []
    for i in range(2):
        old = o_ref[:, 16 * i : 16 * i + 16, :]
        first = old[:, 0, :]
        part = slice(n * i, n * i + n)
        mixed, lse_new = merge(first, swap(first), out[part], lse[part])
        first = jnp.where(lane_is_low(first.shape), mixed, swap(lse_new))
        halves.append(jnp.where(row == 0, first[:, None, :], old))
    block = jnp.concatenate(halves, axis=1)
    high, mid, tail = split(block)
    lane = lax.broadcasted_iota(jnp.int32, block.shape, 2)
    last = jnp.where(lane == LSE_LANE, high, jnp.where(lane == LSE_LANE + 1, mid, tail))
    send = jnp.where(lane < 64, high, jnp.where(lane < LSE_LANE, swap(mid), last))
    ret_ref[...] = send.astype(BF16)


def split(x):
    def leading(y):
        scaled = y * 65537.0
        return scaled - (scaled - y)

    high = leading(x)
    rest = x - high
    mid = leading(rest)
    return high, mid, rest - mid


def local_kernel(start, q_hbm, k_hbm, v_hbm, *rest):
    o_ref, buf, sem, out_scr, lse_scr = rest[-5:]
    step, steps = pl.program_id(0), pl.num_programs(0)
    rows = q_hbm.shape[0]
    groups = rows // 16

    def copies(pair):
        lanes, slot = pl.ds(pl.multiple_of((start + pair) * 128, 128), 128), lax.rem(pair, 2)
        return [
            pltpu.make_async_copy(hbm.at[:, lanes], buf.at[slot, i], sem.at[slot, i])
            for i, hbm in enumerate((q_hbm, k_hbm, v_hbm))
        ]

    @pl.when(step == 0)
    def _():
        for copy in copies(step):
            copy.start()

    @pl.when(step + 1 < steps)
    def _():
        for copy in copies(step + 1):
            copy.start()

    for copy in copies(step):
        copy.wait()
    slot = lax.rem(step, 2)
    k, v = buf[slot, 1], buf[slot, 2]
    tall = rows // 2
    low = lane_is_low((tall, 128))
    parts = [slice(i * tall, i * tall + tall) for i in range(2)]
    scores = {}
    for i, part in enumerate(parts):
        q = buf[slot, 0, part, :]
        for half in range(2):
            query = jnp.where(low == (half == 0), q, jnp.zeros_like(q))
            scores[i, half] = lax.dot_general(query, k, NT, preferred_element_type=F32)
    for i, part in enumerate(parts):
        outs, lses = [], []
        for half in range(2):
            probs, total, lse = soft(scores[i, half])
            outs.append(jnp.dot(probs, v, preferred_element_type=F32) / total)
            lses.append(lse)
        out = jnp.where(low, outs[0], outs[1])
        out_scr[part, :] = out
        lse_scr[part, :] = jnp.where(low, lses[0], lses[1])
        o_ref[part, :] = out.astype(BF16)
    lowr = lane_is_low((groups, 128))
    even = pl.ds(2 * (start + step), groups, stride=16)
    odd = pl.ds(2 * (start + step) + 1, groups, stride=16)
    at = rows
    for scr in (out_scr, lse_scr):
        for piece in split(jnp.where(lowr, scr[even, :], scr[odd, :])):
            o_ref[at : at + groups, :] = piece.astype(BF16)
            at += groups


def finish_kernel(period, n_row, local, r_ref, w_ref, out_hbm, buf, out_sem):
    rows, width = out_hbm.shape
    groups = rows // period
    n = r_ref.shape[0]
    low = lane_is_low((groups, 128))
    backs = [r_ref[slot_of(head, n_row, n)] for head in range(HEADS)]
    source = lax.broadcasted_iota(jnp.int32, (128, 128), 0)
    lse_all = jnp.dot(
        jnp.concatenate(backs, axis=0), (source >= LSE_LANE).astype(BF16), preferred_element_type=F32
    )
    has_low = lax.broadcasted_iota(jnp.int32, (groups, 128), 1) < LSE_LANE - 64
    remote = []
    for pair in range(HEADS // 2):
        outs = [backs[2 * pair + half].astype(F32) for half in range(2)]
        outs = [o + jnp.where(has_low, swap(o), 0.0) for o in outs]
        at = 2 * pair * groups
        lse = [lse_all[at + half * groups : at + (half + 1) * groups] for half in range(2)]
        remote.append((jnp.where(low, outs[0], swap(outs[1])), jnp.where(low, lse[0], lse[1])))
    blocks = []
    for pair in range(HEADS // 2):
        lanes = slice(pair * 128, pair * 128 + 128)
        pieces = [
            local[rows + i * groups : rows + (i + 1) * groups, lanes].astype(F32) for i in range(6)
        ]
        out_a, lse_a = (pieces[i] + pieces[i + 1] + pieces[i + 2] for i in (0, 3))
        blocks.append(merge(out_a, lse_a, *remote[pair])[0])
    merged = jnp.concatenate(blocks, axis=1)
    keep = chosen_lanes(period, width)[None]
    chunks = buf.shape[0]
    tall, wide = rows // chunks, groups // chunks
    copies = []
    for c in range(chunks):
        part = slice(c * tall, c * tall + tall)
        own = local[part, :].astype(F32).reshape(wide, period, width)
        mixed = jnp.where(keep, merged[c * wide : c * wide + wide][:, None, :], own)
        mixed = mixed.reshape(tall, width).astype(BF16)
        buf[c] = jnp.dot(mixed, w_ref[...], preferred_element_type=F32).astype(BF16)
        copy = pltpu.make_async_copy(buf.at[c], out_hbm.at[pl.ds(c * tall, tall)], out_sem.at[c])
        copy.start()
        copies.append(copy)
    for copy in copies:
        copy.wait()


def shards(queries, keys, values, out_weight):
    n_row, n_col = lax.axis_size("row"), lax.axis_size("col")
    rows, width = queries.shape
    groups = rows // n_col
    shape = jax.ShapeDtypeStruct

    def call(kernel, out, mib=16, **kw):
        params = pltpu.CompilerParams(vmem_limit_bytes=mib * 1024 * 1024)
        return pl.pallas_call(kernel, out_shape=out, compiler_params=params, **kw)

    anywhere = pl.BlockSpec(memory_space=pl.ANY)
    distant = pl.BlockSpec(memory_space=pltpu.HBM)
    whole = pl.BlockSpec(memory_space=pltpu.VMEM)
    packed = call(
        lambda *refs: pack_kernel(n_col, n_row, *refs),
        shape((n_col, groups * 3 // 2, 128), BF16),
        mib=56,
        in_specs=[distant] * 3,
        out_specs=anywhere,
        scratch_shapes=[
            pltpu.VMEM((3, rows, width), BF16),
            pltpu.SemaphoreType.DMA((3,)),
            pltpu.VMEM((n_col, groups * 3 // 2, 128), BF16),
            pltpu.SemaphoreType.DMA((2,)),
        ],
    )(queries, keys, values)
    def local(start, count, inputs, aliases):
        pairs = rows * rows * 2 * count
        return call(
            lambda *refs: local_kernel(start, *refs),
            shape((rows + 6 * groups, width), BF16),
            mib=54,
            grid=(count,),
            in_specs=[distant] * 3 + [anywhere] * (len(inputs) - 3),
            out_specs=pl.BlockSpec((rows + 6 * groups, 128), lambda i: (0, start + i)),
            scratch_shapes=[
                pltpu.VMEM((2, 3, rows, 128), BF16),
                pltpu.SemaphoreType.DMA((2, 3)),
                pltpu.VMEM((rows, 128), F32),
                pltpu.VMEM((rows, 128), F32),
            ],
            input_output_aliases=aliases,
            cost_estimate=pl.CostEstimate(
                flops=pairs * 1024, bytes_accessed=count * rows * 128 * 10, transcendentals=pairs
            ),
        )(*inputs)

    inputs = (queries, keys, values)
    packed, *inputs = lax.optimization_barrier((packed, *inputs))
    mine = lax.all_to_all(packed, "col", 0, 0, axis_index_groups=col_order(n_col))
    early = HEADS // 3
    first = local(0, early, inputs, {})
    mine, first = lax.optimization_barrier((mine, first))
    top_own = call(middle_kernel, shape((n_row, 2 * n_col, 128), BF16))(mine)
    top_own, mine, first, *inputs = lax.optimization_barrier((top_own, mine, first, *inputs))
    owners = owner_groups(n_row, n_col)
    top_all = lax.all_to_all(top_own, ("row", "col"), 0, 0, axis_index_groups=owners)
    second = local(early, HEADS // 2 - early, (*inputs, first), {3: 0})
    mine, second = lax.optimization_barrier((mine, second))
    segment = call(segment_kernel, shape((n_col, groups, 128), F32))(mine)
    top_all, segment = lax.optimization_barrier((top_all, segment))
    ret = call(
        sequence_kernel,
        shape((n_col, groups, 128), BF16),
        cost_estimate=pl.CostEstimate(flops=10**10, bytes_accessed=10**6, transcendentals=0),
    )(mine, top_all, segment)
    back = lax.all_to_all(ret, "col", 0, 0, axis_index_groups=col_order(n_col))
    return call(
        lambda *refs: finish_kernel(n_col, n_row, *refs),
        shape((rows, width), BF16),
        in_specs=[whole] * 3,
        out_specs=anywhere,
        scratch_shapes=[pltpu.VMEM((4, rows // 4, width), BF16), pltpu.SemaphoreType.DMA((4,))],
    )(second, back, out_weight)


def solution(mesh):
    placed = (P(("row", "col"), None), P(("row", "col"), None), P(("row", "col"), None), P())
    return jax.shard_map(
        shards, mesh=mesh, in_specs=placed, out_specs=P(("row", "col"), None), check_vma=False
    )
```
